32 devices in a mesh: dp: 16 (over z, x, core), expert: 2 (over y).
Axes of the slice: x: 2, y: 2, z: 4, core: 2. Of those that a mesh axis runs over, the one named last changes fastest.
Arguments:
- tokens: bfloat16 [8192, 2560], P(('dp', 'expert')), may hold values from -6 to 6
- routes: int32 [8192, 1], P(('dp', 'expert')), may hold values from 0 to 1; in each aligned block of 256 rows (0 to 255, 256 to 511, ...) at most 160 rows name the same one
- gate_levels: int32 [8192, 1], P(('dp', 'expert')), may hold values from 1 to 64
- w_gate: bfloat16 [2, 2560, 768], P('expert', 'dp'), may hold values from -0.125 to 0.125
- w_up: bfloat16 [2, 2560, 768], P('expert', 'dp'), may hold values from -0.125 to 0.125
- w_down: bfloat16 [2, 2560, 768], P('expert', 'dp'), may hold values from -0.21875 to 0.21875
- grad_out: bfloat16 [8192, 2560], P(('dp', 'expert')), may hold values from -6 to 6
Outputs:
- moe_out: bfloat16 [8192, 2560], P(('dp', 'expert'))
- grad_tokens: bfloat16 [8192, 2560], P(('dp', 'expert'))
- grad_gate: float32 [2, 2560, 768], P('expert', 'dp')
- grad_up: float32 [2, 2560, 768], P('expert', 'dp')
- grad_down: float32 [2, 2560, 768], P('expert', 'dp')
The draws below stay inside these ranges and needn't reach their ends.
Inputs may be any that keep to these rules, and one draw needn't show every extreme that they name: `routes`: among the rows of one device, no expert is named by more than 160 tokens, a bound that some block reaches.
All inputs are finite; a program needn't handle non-finite values.
Results may differ from the reference program's by a relative error of at most 0.019.
Values may be sent and summed in bfloat16 or wider, within the bound.
A program may use at most 128 MiB of HBM per device.

```python
import math
import jax
import jax.numpy as jnp
import numpy as np
from jax import lax

D = 2560
FF = 768
TOP = 1
TOK_DEV = 256
EXPERTS = 2
CAP = 160
TOKENS = 8192
N_DP = 16
N_EXPERT = 2


def place_ends(values, key, least, high):
    spot = [jax.random.randint(jax.random.fold_in(key, axis), (), 0, length) for axis, length in enumerate(values.shape)]
    widest = values.shape.index(max(values.shape))
    next_to = spot[:widest] + [(spot[widest] + 1) % values.shape[widest]] + spot[widest + 1:]
    return values.at[tuple(spot)].set(least).at[tuple(next_to)].set(high)


def with_spikes(array, rng, source, target, blocks, factor):
    owner, partner = [(jnp.arange(array.shape[dim]) // (array.shape[dim] // blocks)).reshape([-1 if axis == dim else 1 for axis in range(array.ndim)]) for dim in (source, target)]
    chosen = jax.random.permutation(rng, blocks)[partner]
    strong = (owner == chosen) | (owner == (partner + blocks // 2) % blocks)
    return jnp.where(strong, factor * array, array)


def shard_levels(key, extent, cuts, smallest, top_value):
    gain = 1.0
    for position, parts in cuts:
        heights = jax.random.uniform(jax.random.fold_in(jax.random.fold_in(key, 6), position), (parts,), jnp.float32, smallest / len(cuts), top_value / len(cuts))
        gain = gain * jnp.repeat(jnp.exp(heights), extent[position] // parts).reshape((-1,) + (1,) * (len(extent) - 1 - position))
    return gain


def deal_out(own_key, own, number, rows, count, top, most, slope):
    ranking = jax.random.permutation(own_key, count)
    packed, ordinary = portions_of(count, rows * top, most, slope, True), portions_of(count, rows * top, most, slope, False)
    places = jnp.arange(count)

    def named(sizes, turn):
        used = int((sizes > 0).sum())
        fixed = max(1, used // 4)
        passed = fixed + (places - fixed + turn * (used - fixed)) % max(1, count - fixed)
        return jnp.zeros((count,), jnp.int32).at[ranking[jnp.where(places < fixed, places, passed)]].set(jnp.asarray(sizes, jnp.int32))

    sizes = jnp.where(number % 4 == 0, named(packed, number // 4), named(ordinary, number - number // 4 - 1))
    mixed = jax.random.permutation(jax.random.fold_in(own, 3), count)
    donor, sink = mixed[0:count // 2 * 2:2], mixed[1:count // 2 * 2:2]
    margin = jnp.minimum(sizes[donor] - 1, most - sizes[sink]) // 2
    margin = jnp.where((donor == ranking[0]) | (sink == ranking[0]) | (sizes[sink] == 0), 0, jnp.maximum(margin, 0))
    passed = jax.random.randint(jax.random.fold_in(own, 4), (count // 2,), 0, 1 << 20) % (margin + 1)
    sizes = sizes.at[donor].add(-passed).at[sink].add(passed)
    labels = jnp.searchsorted(jnp.cumsum(sizes), jnp.arange(rows * top), side="right").astype(jnp.int32)
    grid = labels.reshape(top, rows).T
    grid = grid[jax.random.permutation(jax.random.fold_in(own, 1), rows)]
    turn = jax.random.randint(jax.random.fold_in(own, 2), (rows, 1), 0, top)
    return jnp.take_along_axis(grid, (jnp.arange(top)[None, :] + turn) % top, axis=1)


def portions_of(amount, total, limit, lean, full):
    loads = [(1 << 20) // math.isqrt(grade ** lean) + 1 for grade in range(1, amount + 1)]
    largest = limit if full else min(limit, max(-(-total // amount), total * loads[0] // sum(loads)))
    least = 1 if total - largest >= amount - 1 else 0
    given, surplus = [largest] + [least] * (amount - 1), total - largest - least * (amount - 1)
    while surplus > 0:
        movable = [i for i in range(1, amount) if given[i] < largest] or [i for i in range(1, amount) if given[i] < limit]
        pool, remaining = sum([loads[i] for i in movable]), surplus
        for i in movable:
            extra = min(limit - given[i], max(1, remaining * loads[i] // pool), surplus)
            given[i] = given[i] + extra
            surplus = surplus - extra
    return np.array(given)


def centred(stream_key, extent, scale, reach, cuts=(), held_as=jnp.bfloat16):
    gain = shard_levels(stream_key, extent, cuts, -0.22, 0.18) if cuts else 1.0
    values = jax.random.normal(stream_key, extent, jnp.float32) * scale * gain
    return jnp.minimum(jnp.maximum(values, -reach), reach).astype(held_as)


def heavy_noise(rng, shape, deviation, limit, shards, heavy, kind=jnp.bfloat16):
    entries = deviation * jax.random.normal(rng, shape, jnp.float32)
    if shards:
        entries = entries * shard_levels(rng, shape, shards, -0.22, 0.18)
    return jnp.clip(with_spikes(entries, jax.random.fold_in(rng, 3), *heavy), -limit, limit).astype(kind)


def setup_inputs(seed: int = 0) -> dict:
    key_of = jax.random.split(jax.random.key(seed), 8)
    tokens = heavy_noise(key_of[0], (TOKENS, D), 1.0, 6.0, ((0, 32),), (0, 1, 32, 2.75))
    routes_keys = jax.random.split(jax.random.fold_in(key_of[1], 1), TOKENS // TOK_DEV)
    routes_turns = jax.random.permutation(jax.random.fold_in(key_of[1], 3), TOKENS // TOK_DEV)
    routes = jax.vmap(lambda own, number: deal_out(jax.random.fold_in(key_of[1], 2), own, number, TOK_DEV, EXPERTS, TOP, CAP, 2))(routes_keys, routes_turns).reshape((TOKENS, TOP))
    gate_levels = place_ends(jax.random.randint(key_of[2], (TOKENS, TOP), 1, 65), jax.random.fold_in(key_of[2], 1), 1, 64).astype(jnp.int32)
    w_gate = centred(key_of[3], (EXPERTS, D, FF), D ** -0.5, 0.125, ((0, 2), (1, 16)))
    w_up = centred(key_of[4], (EXPERTS, D, FF), D ** -0.5, 0.125, ((0, 2), (1, 16)))
    w_down = centred(key_of[5], (EXPERTS, D, FF), FF ** -0.5, 0.21875, ((0, 2), (1, 16)))
    grad_out = heavy_noise(key_of[6], (TOKENS, D), 1.0, 6.0, ((0, 32),), (0, 1, 32, 2.75))
    return {"tokens": tokens, "routes": routes, "gate_levels": gate_levels, "w_gate": w_gate, "w_up": w_up, "w_down": w_down, "grad_out": grad_out}


def contract_last(matrix_a, matrix_b):
    return lax.dot_general(matrix_a, matrix_b, (((1,), (1,)), ((), ())), preferred_element_type=jnp.float32)


def contract_first(matrix_a, matrix_b):
    return lax.dot_general(matrix_a, matrix_b, (((0,), (0,)), ((), ())), preferred_element_type=jnp.float32)


def block_ranks(expert_of):
    onehot = (expert_of[:, None] == jnp.arange(EXPERTS, dtype=jnp.int32)[None, :]).astype(jnp.int32)
    earlier = jnp.cumsum(onehot, axis=0) - onehot
    return jnp.sum(earlier * onehot, axis=1).astype(jnp.int32)


def place_rows(values, expert_of, slot_rank):
    return jnp.zeros((EXPERTS, CAP, D), jnp.bfloat16).at[expert_of, slot_rank].set(values)


def pick_rows(stacked, expert_of, slot_rank):
    return stacked[expert_of, slot_rank]


def expert_pass(received, grad_rows, gate_full, up_full, down_full):
    act_gate = jnp.dot(received, gate_full, preferred_element_type=jnp.float32)
    act_up = jnp.dot(received, up_full, preferred_element_type=jnp.float32)
    sigmoid_gate = jax.nn.sigmoid(act_gate)
    silu_gate = act_gate * sigmoid_gate
    hidden = (silu_gate * act_up).astype(jnp.bfloat16)
    expert_out = contract_last(hidden, down_full).astype(jnp.bfloat16)
    hidden_grad = jnp.dot(grad_rows, down_full, preferred_element_type=jnp.float32)
    gate_delta = (hidden_grad * act_up * sigmoid_gate * (1.0 + act_gate * (1.0 - sigmoid_gate))).astype(jnp.bfloat16)
    up_delta = (hidden_grad * silu_gate).astype(jnp.bfloat16)
    token_grad = (contract_last(gate_delta, gate_full) + contract_last(up_delta, up_full)).astype(jnp.bfloat16)
    part_gate = contract_first(received, gate_delta).astype(jnp.bfloat16)
    part_up = contract_first(received, up_delta).astype(jnp.bfloat16)
    part_down = contract_first(grad_rows, hidden).astype(jnp.bfloat16)
    return expert_out, token_grad, part_gate, part_up, part_down


def reference(tokens, routes, gate_levels, w_gate, w_up, w_down, grad_out):
    tok_blocks = tokens.reshape(N_DP, N_EXPERT, TOK_DEV, D)
    route_blocks = routes.reshape(N_DP, N_EXPERT, TOK_DEV)
    level_blocks = gate_levels.reshape(N_DP, N_EXPERT, TOK_DEV, 1)
    grad_blocks = grad_out.reshape(N_DP, N_EXPERT, TOK_DEV, D)

    def row_pass(carry, inputs):
        tok_row, route_row, level_row, grad_row = inputs
        rank_row = jax.vmap(block_ranks)(route_row)
        gate_weight = level_row.astype(jnp.float32) / 64.0
        out_grad = (gate_weight * grad_row.astype(jnp.float32)).astype(jnp.bfloat16)
        tok_place = jax.vmap(place_rows)(tok_row, route_row, rank_row)
        grad_place = jax.vmap(place_rows)(out_grad, route_row, rank_row)
        outs_list = []
        grads_list = []
        gate_parts = []
        up_parts = []
        down_parts = []
        for expert in range(EXPERTS):
            received = tok_place[:, expert].reshape(N_EXPERT * CAP, D)
            grad_rows = grad_place[:, expert].reshape(N_EXPERT * CAP, D)
            results = expert_pass(received, grad_rows, w_gate[expert], w_up[expert], w_down[expert])
            outs_list.append(results[0].reshape(N_EXPERT, CAP, D))
            grads_list.append(results[1].reshape(N_EXPERT, CAP, D))
            gate_parts.append(results[2])
            up_parts.append(results[3])
            down_parts.append(results[4])
        out_stack = jnp.stack(outs_list, axis=1)
        grad_stack = jnp.stack(grads_list, axis=1)
        expert_out = jax.vmap(pick_rows)(out_stack, route_row, rank_row)
        moe_row = (gate_weight * expert_out.astype(jnp.float32)).astype(jnp.bfloat16)
        grad_row_out = jax.vmap(pick_rows)(grad_stack, route_row, rank_row)
        new_carry = (carry[0] + jnp.stack(gate_parts).astype(jnp.float32),
                     carry[1] + jnp.stack(up_parts).astype(jnp.float32),
                     carry[2] + jnp.stack(down_parts).astype(jnp.float32))
        return new_carry, (moe_row, grad_row_out)

    zeros = jnp.zeros((EXPERTS, D, FF), jnp.float32)
    sums, rows_out = lax.scan(row_pass, (zeros, zeros, zeros), (tok_blocks, route_blocks, level_blocks, grad_blocks))
    moe_out = rows_out[0].reshape(TOKENS, D)
    grad_tokens = rows_out[1].reshape(TOKENS, D)
    return moe_out, grad_tokens, sums[0], sums[1], sums[2]
```

```python
import functools

import jax
import jax.numpy as jnp
from jax import lax
from jax.experimental import pallas as pl
from jax.experimental.pallas import tpu as pltpu
from jax.sharding import PartitionSpec as P

TOP = 1
MESH = pl.DeviceIdType.MESH
VMEM_LIMIT = 58 * 1024 * 1024


def contract_last(matrix_a, matrix_b):
    return lax.dot_general(
        matrix_a, matrix_b, (((1,), (1,)), ((), ())), preferred_element_type=jnp.float32
    )


def contract_first(matrix_a, matrix_b):
    return lax.dot_general(
        matrix_a, matrix_b, (((0,), (0,)), ((), ())), preferred_element_type=jnp.float32
    )


class Sent:
    def __init__(self):
        self.made = []

    def start(self, make, cond=None):
        self.made.append((make, cond))
        run(lambda: make().start(), cond)

    def finish(self):
        for make, cond in self.made:
            run(lambda make=make: make().wait_send(), cond)


def run(body, cond=None):
    if cond is None:
        body()
    else:
        pl.when(cond)(body)


def places(lines, cross):
    dp = lax.axis_index("dp")
    return dp, lax.axis_index("expert"), dp // (2 * cross), (dp // 2) % cross, dp % 2


def greet(lines, cross, experts):
    dp, own, z, x, c = places(lines, cross)
    barrier = pltpu.get_barrier_semaphore()

    def hello(to_dp, to_expert):
        pl.semaphore_signal(barrier, inc=1, device_id=(to_dp, to_expert), device_id_type=MESH)

    run(lambda: hello(dp + 2 * cross, own), z < lines - 1)
    run(lambda: hello(dp - 2 * cross, own), z > 0)
    for o in range(1, cross):
        hello((z * cross + (x + o) % cross) * 2 + c, own)
    hello(dp + 1 - 2 * c, own)
    for o in range(1, experts):
        hello(dp, (own + o) % experts)
    up = jnp.where(z < lines - 1, 1, 0)
    down = jnp.where(z > 0, 1, 0)
    pl.semaphore_wait(barrier, up + down + (cross - 1) + 1 + (experts - 1))


def gather_kernel(lines, cross, experts, *refs):
    shards, blocks, fulls, landed = refs[0:3], refs[3:5], refs[5:8], refs[8:10]
    z_send, z_recv, x_send, x_recv, c_send, c_recv, y_send, y_recv, own_sem = refs[10:]
    dp, own, z, x, c = places(lines, cross)
    greet(lines, cross, experts)
    sent = Sent()
    local = []

    def at(q, r, s):
        return (q * cross + r) * 2 + s

    def copy(src, dst, send, recv, to_dp, to_expert):
        return pltpu.make_async_remote_copy(
            src_ref=src, dst_ref=dst, send_sem=send, recv_sem=recv,
            device_id=(to_dp, to_expert), device_id_type=MESH,
        )

    def y_copy(t, o):
        to = (own + o) % experts
        return copy(blocks[t].at[to], landed[t].at[own], y_send.at[t, o], y_recv.at[t, o], dp, to)

    def z_copy(k, q, step, src):
        side = 0 if step > 0 else 1
        return copy(src, fulls[k].at[at(q, x, c)], z_send.at[side, q, k], z_recv.at[q, k],
                    at(z + step, x, c), own)

    def x_copy(k, q, o, src):
        return copy(src, fulls[k].at[at(q, x, c)], x_send.at[q, o, k], x_recv.at[q, o, k],
                    at(z, (x + o) % cross, c), own)

    def c_copy(k, q, r, src):
        return copy(src, fulls[k].at[at(q, r, c)], c_send.at[q, r, k], c_recv.at[q, r, k],
                    at(z, x, 1 - c), own)

    bind = functools.partial
    for k in range(3):
        sent.start(bind(lambda k: z_copy(k, z, 1, shards[k]), k), z < lines - 1)
        sent.start(bind(lambda k: z_copy(k, z, -1, shards[k]), k), z > 0)
        for o in range(1, cross):
            sent.start(bind(lambda k, o: x_copy(k, z, o, shards[k]), k, o))
        sent.start(bind(lambda k: c_copy(k, z, x, shards[k]), k))
        if k == 0:
            for o in range(1, experts):
                sent.start(bind(lambda o: y_copy(0, o), o))
    for t in range(1, 2):
        for o in range(1, experts):
            sent.start(functools.partial(y_copy, t, o))
    for k in range(3):
        local.append(pltpu.make_async_copy(shards[k], fulls[k].at[dp], own_sem.at[k]))
    for t in range(2):
        local.append(pltpu.make_async_copy(blocks[t].at[own], landed[t].at[own], own_sem.at[3 + t]))
    for each in local:
        each.start()

    def from_z(k, q, step, cond):
        held = lambda: fulls[k].at[at(q, x, c)]
        run(lambda: z_copy(k, q, step, held()).wait_recv(), cond)
        onward = (z < lines - 1) if step > 0 else (z > 0)
        sent.start(lambda: z_copy(k, q, step, held()), cond & onward)
        for o in range(1, cross):
            sent.start(bind(lambda o: x_copy(k, q, o, held()), o), cond)
        sent.start(lambda: c_copy(k, q, x, held()), cond)

    def from_x(k, q, cond):
        for o in range(1, cross):
            r = (x - o + cross) % cross
            held = bind(lambda r: fulls[k].at[at(q, r, c)], r)
            run(lambda: copy(held(), held(), x_send.at[q, o, k], x_recv.at[q, o, k], dp + 1 - 2 * c, own).wait_recv(), cond)
            sent.start(bind(lambda r, held: c_copy(k, q, r, held()), r, held), cond)

    for s in range(1, lines + 1):
        for k in range(3):
            if s < lines:
                from_z(k, z - s, 1, z >= s)
                from_z(k, z + s, -1, z + s < lines)
            if s == 1:
                from_x(k, z, None)
            else:
                from_x(k, z - (s - 1), z >= s - 1)
                from_x(k, z + (s - 1), z + s - 1 < lines)
    for k in range(3):
        for q in range(lines):
            for r in range(cross):
                held = fulls[k].at[at(q, r, 1 - c)]
                copy(held, held, c_send.at[q, r, k], c_recv.at[q, r, k], dp + 1 - 2 * c, own).wait_recv()
    for t in range(2):
        for o in range(1, experts):
            held = landed[t].at[(own - o + experts) % experts]
            copy(held, held, y_send.at[t, o], y_recv.at[t, o], dp, (own + o) % experts).wait_recv()
    for each in local:
        each.wait()
    sent.finish()


def scatter_kernel(lines, cross, experts, *refs):
    parts, blocks, totals, landed = refs[0:3], refs[3:5], refs[5:8], refs[8:10]
    c_buf, x_buf, z_buf, stage = refs[10:14]
    z_send, z_recv, x_send, x_recv, c_send, c_recv, y_send, y_recv, own_sem = refs[14:]
    dp, own, z, x, c = places(lines, cross)
    greet(lines, cross, experts)
    sent = Sent()
    bind = functools.partial

    def at(q, r, s):
        return (q * cross + r) * 2 + s

    def copy(src, dst, send, recv, to_dp, to_expert):
        return pltpu.make_async_remote_copy(
            src_ref=src, dst_ref=dst, send_sem=send, recv_sem=recv,
            device_id=(to_dp, to_expert), device_id_type=MESH,
        )

    def y_copy(t, o):
        to = (own + o) % experts
        return copy(blocks[t].at[to], landed[t].at[own], y_send.at[t, o], y_recv.at[t, o], dp, to)

    def c_copy(k, q, r):
        return copy(parts[k].at[at(q, r, 1 - c)], c_buf.at[k, q, r], c_send.at[k, q, r],
                    c_recv.at[k, q, r], dp + 1 - 2 * c, own)

    def x_copy(k, q, o):
        to = (x + o) % cross
        return copy(c_buf.at[k, q, to], x_buf.at[k, q, o], x_send.at[k, q, o],
                    x_recv.at[k, q, o], at(z, to, c), own)

    def z_copy(k, q, step):
        side = 0 if step > 0 else 1
        return copy(stage.at[k, q], z_buf.at[side, k, q], z_send.at[side, k, q],
                    z_recv.at[side, k, q], at(z + step, x, c), own)

    order = []
    for d in range(lines - 1, 0, -1):
        order.append((d, z + d, z + d < lines))
        order.append((-d, z - d, z >= d))
    order.append((0, z, None))

    for t in range(2):
        for o in range(1, experts):
            sent.start(bind(y_copy, t, o))
    local = []
    for t in range(2):
        local.append(pltpu.make_async_copy(blocks[t].at[own], landed[t].at[own], own_sem.at[t]))
    for each in local:
        each.start()
    for d, q, cond in order:
        for k in range(3):
            for o in range(cross):
                sent.start(bind(lambda k, q, o: c_copy(k, q, (x + 1 + o) % cross), k, q, o), cond)

    def pair(k, q, r):
        c_copy(k, q, r).wait_recv()
        return parts[k][at(q, r, c)].astype(jnp.float32) + c_buf[k, q, r].astype(jnp.float32)

    for d, q, cond in order:
        for k in range(3):
            for o in range(1, cross):
                def body(k=k, q=q, o=o):
                    r = (x + o) % cross
                    c_buf[k, q, r] = pair(k, q, r).astype(jnp.bfloat16)
                run(body, cond)
                sent.start(bind(x_copy, k, q, o), cond)

    for d, q, cond in order:
        for k in range(3):
            def body(k=k, q=q, d=d):
                total = pair(k, q, x)
                for o in range(1, cross):
                    x_copy(k, q, o).wait_recv()
                    total = total + x_buf[k, q, o].astype(jnp.float32)
                if d == 0:
                    totals[k][...] = total
                else:
                    stage[k, q] = total.astype(jnp.bfloat16)
            run(body, cond)
            if d >= 0:
                def rest(k=k, q=q, d=d):
                    z_copy(k, q, 1).wait_recv()
                    more = z_buf[0, k, q].astype(jnp.float32)
                    if d == 0:
                        totals[k][...] += more
                    else:
                        stage[k, q] = (stage[k, q].astype(jnp.float32) + more).astype(jnp.bfloat16)
                run(rest, (z > 0) if cond is None else cond & (z > 0))
            if d <= 0:
                def rest(k=k, q=q, d=d):
                    z_copy(k, q, -1).wait_recv()
                    more = z_buf[1, k, q].astype(jnp.float32)
                    if d == 0:
                        totals[k][...] += more
                    else:
                        stage[k, q] = (stage[k, q].astype(jnp.float32) + more).astype(jnp.bfloat16)
                run(rest, (z < lines - 1) if cond is None else cond & (z < lines - 1))
            if d != 0:
                sent.start(bind(z_copy, k, q, 1 if d > 0 else -1), cond)
    for t in range(2):
        for o in range(1, experts):
            held = landed[t].at[(own - o + experts) % experts]
            copy(held, held, y_send.at[t, o], y_recv.at[t, o], dp, (own + o) % experts).wait_recv()
    for each in local:
        each.wait()
    sent.finish()


def semaphores(lines, cross, experts, own):
    dma = pltpu.SemaphoreType.DMA
    return dma, [dma((2, experts)), dma((2, experts)), dma((own,))]


def gather_all(lines, cross, experts, trio, blocks):
    n = lines * cross * 2
    rows, width = trio[0].shape
    dma, last = semaphores(lines, cross, experts, 5)
    anywhere = pl.BlockSpec(memory_space=pl.ANY)
    full = jax.ShapeDtypeStruct((n, rows, width), jnp.bfloat16)
    outs = pl.pallas_call(
        functools.partial(gather_kernel, lines, cross, experts),
        out_shape=[full] * 3 + [jax.ShapeDtypeStruct(b.shape, b.dtype) for b in blocks],
        in_specs=[anywhere] * 5,
        out_specs=[anywhere] * 5,
        scratch_shapes=[dma((2, lines, 3)), dma((lines, 3))]
        + [dma((lines, cross, 3)) for _ in range(4)] + last,
        compiler_params=pltpu.CompilerParams(collective_id=0, has_side_effects=True),
        name="gather_and_exchange",
    )(*trio, *blocks)
    return [f.reshape(n * rows, width) for f in outs[:3]], outs[3:]


def scatter_all(lines, cross, experts, parts, blocks):
    n = lines * cross * 2
    width = parts[0].shape[1]
    rows = parts[0].shape[0] // n
    dma, last = semaphores(lines, cross, experts, 2)
    anywhere = pl.BlockSpec(memory_space=pl.ANY)
    inside = pl.BlockSpec(memory_space=pltpu.VMEM)
    total = jax.ShapeDtypeStruct((rows, width), jnp.float32)
    block = (rows, width)
    outs = pl.pallas_call(
        functools.partial(scatter_kernel, lines, cross, experts),
        out_shape=[total] * 3 + [jax.ShapeDtypeStruct(b.shape, b.dtype) for b in blocks],
        in_specs=[inside] * 3 + [anywhere] * 2,
        out_specs=[inside] * 3 + [anywhere] * 2,
        scratch_shapes=[
            pltpu.VMEM((3, lines, cross) + block, jnp.bfloat16),
            pltpu.VMEM((3, lines, cross) + block, jnp.bfloat16),
            pltpu.VMEM((2, 3, lines) + block, jnp.bfloat16),
            pltpu.VMEM((3, lines) + block, jnp.bfloat16),
            dma((2, 3, lines)), dma((2, 3, lines)),
        ] + [dma((3, lines, cross)) for _ in range(4)] + last,
        compiler_params=pltpu.CompilerParams(
            collective_id=1, has_side_effects=True, vmem_limit_bytes=VMEM_LIMIT
        ),
        name="scatter_and_return",
    )(*[p.reshape(n, rows, width) for p in parts], *blocks)
    return outs[:3], outs[3:]


def shards(lines, cross, tokens, routes, gate_levels, w_gate, w_up, w_down, grad_out):
    experts = lax.axis_size("expert")
    tok_rows = tokens.shape[0]
    model_width = tokens.shape[1]
    capacity = min(tok_rows, tok_rows * TOP * 5 // (4 * experts))
    slot_count = experts * capacity
    expert_of = routes[:, 0]
    onehot = (expert_of[:, None] == jnp.arange(experts, dtype=jnp.int32)[None, :]).astype(jnp.bfloat16)
    place = jnp.arange(tok_rows, dtype=jnp.int32)
    earlier = jnp.dot(
        (place[:, None] > place[None, :]).astype(jnp.bfloat16), onehot,
        preferred_element_type=jnp.float32,
    )
    slot_rank = jnp.sum(earlier * onehot.astype(jnp.float32), axis=1).astype(jnp.int32)
    slot_index = expert_of * capacity + slot_rank
    to_slot = (slot_index[:, None] == jnp.arange(slot_count, dtype=jnp.int32)[None, :]).astype(
        jnp.bfloat16
    )
    gate_weight = gate_levels.astype(jnp.float32) / 64.0

    def pack_rows(values):
        return contract_first(to_slot, values).astype(jnp.bfloat16).reshape(
            experts, capacity, model_width
        )

    def unpack_rows(values):
        return jnp.dot(
            to_slot, values.reshape(slot_count, model_width), preferred_element_type=jnp.float32
        )

    out_grad = (gate_weight * grad_out.astype(jnp.float32)).astype(jnp.bfloat16)
    (gate_full, up_full, down_full), (received, grad_rows) = gather_all(
        lines, cross, experts, (w_gate[0], w_up[0], w_down[0]),
        (pack_rows(tokens), pack_rows(out_grad)),
    )
    received = received.reshape(slot_count, model_width)
    grad_rows = grad_rows.reshape(slot_count, model_width)
    act_gate = jnp.dot(received, gate_full, preferred_element_type=jnp.float32)
    act_up = jnp.dot(received, up_full, preferred_element_type=jnp.float32)
    sigmoid_gate = jax.nn.sigmoid(act_gate)
    silu_gate = act_gate * sigmoid_gate
    hidden = (silu_gate * act_up).astype(jnp.bfloat16)
    expert_out = contract_last(hidden, down_full).astype(jnp.bfloat16)
    hidden_grad = jnp.dot(grad_rows, down_full, preferred_element_type=jnp.float32)
    gate_delta = (
        hidden_grad * act_up * sigmoid_gate * (1.0 + act_gate * (1.0 - sigmoid_gate))
    ).astype(jnp.bfloat16)
    up_delta = (hidden_grad * silu_gate).astype(jnp.bfloat16)
    token_grad = (contract_last(gate_delta, gate_full) + contract_last(up_delta, up_full)).astype(
        jnp.bfloat16
    )
    part_gate = contract_first(received, gate_delta).astype(jnp.bfloat16)
    part_up = contract_first(received, up_delta).astype(jnp.bfloat16)
    part_down = contract_first(grad_rows, hidden).astype(jnp.bfloat16)
    (grad_gate, grad_up, grad_down), (returned, arrived) = scatter_all(
        lines, cross, experts, (part_gate, part_up, part_down),
        (expert_out.reshape(experts, capacity, model_width),
         token_grad.reshape(experts, capacity, model_width)),
    )
    moe_out = (gate_weight * unpack_rows(returned)).astype(jnp.bfloat16)
    grad_tokens = unpack_rows(arrived).astype(jnp.bfloat16)
    return (moe_out, grad_tokens, grad_gate[None], grad_up[None], grad_down[None])


def solution(mesh):
    chips = mesh.shape["dp"] // 2
    lines = 4 if chips % 4 == 0 else chips
    in_specs = (
        P(("dp", "expert"), None),
        P(("dp", "expert"), None),
        P(("dp", "expert"), None),
        P("expert", "dp", None),
        P("expert", "dp", None),
        P("expert", "dp", None),
        P(("dp", "expert"), None),
    )
    out_specs = (
        P(("dp", "expert"), None),
        P(("dp", "expert"), None),
        P("expert", "dp", None),
        P("expert", "dp", None),
        P("expert", "dp", None),
    )
    return jax.shard_map(
        functools.partial(shards, lines, chips // lines),
        mesh=mesh, in_specs=in_specs, out_specs=out_specs, check_vma=False,
    )
```

```python
import functools

import jax
import jax.numpy as jnp
from jax import lax
from jax.experimental import pallas as pl
from jax.experimental.pallas import tpu as pltpu
from jax.sharding import PartitionSpec as P

TOP = 1
MESH = pl.DeviceIdType.MESH
VMEM_LIMIT = 62 * 1024 * 1024


def contract_last(matrix_a, matrix_b):
    return lax.dot_general(
        matrix_a, matrix_b, (((1,), (1,)), ((), ())), preferred_element_type=jnp.float32
    )


def contract_first(matrix_a, matrix_b):
    return lax.dot_general(
        matrix_a, matrix_b, (((0,), (0,)), ((), ())), preferred_element_type=jnp.float32
    )


class Sent:
    def __init__(self):
        self.made = []

    def start(self, make, cond=None):
        self.made.append((make, cond))
        run(lambda: make().start(), cond)

    def finish(self):
        for make, cond in self.made:
            run(lambda make=make: make().wait_send(), cond)


def run(body, cond=None):
    if cond is None:
        body()
    else:
        pl.when(cond)(body)


def places(lines, cross):
    dp = lax.axis_index("dp")
    return dp, lax.axis_index("expert"), dp // (2 * cross), (dp // 2) % cross, dp % 2


def greet(lines, cross, experts):
    dp, own, z, x, c = places(lines, cross)
    barrier = pltpu.get_barrier_semaphore()

    def hello(to_dp, to_expert):
        pl.semaphore_signal(barrier, inc=1, device_id=(to_dp, to_expert), device_id_type=MESH)

    run(lambda: hello(dp + 2 * cross, own), z < lines - 1)
    run(lambda: hello(dp - 2 * cross, own), z > 0)
    for o in range(1, cross):
        hello((z * cross + (x + o) % cross) * 2 + c, own)
    hello(dp + 1 - 2 * c, own)
    for o in range(1, experts):
        hello(dp, (own + o) % experts)
    up = jnp.where(z < lines - 1, 1, 0)
    down = jnp.where(z > 0, 1, 0)
    pl.semaphore_wait(barrier, up + down + (cross - 1) + 1 + (experts - 1))


def layer_kernel(lines, cross, experts, *refs):
    shards, to_slot, tokens, levels, grad_out, totals = refs[0:3], refs[3], refs[4], refs[5], refs[6], refs[7]
    returned = refs[8:10]
    fulls, blocks, landed, outs, acts, deltas, parts, c_buf, x_buf, z_buf, acc = refs[10:21]
    (z_send, z_recv, x_send, x_recv, c_send, c_recv, y_send, y_recv, own_sem,
     rz_send, rz_recv, rx_send, rx_recv, rc_send, rc_recv, ry_send, ry_recv) = refs[21:]
    dp, own, z, x, c = places(lines, cross)
    other = dp + 1 - 2 * c
    per = 2 * cross
    rows, width = fulls.shape[2], fulls.shape[3]
    slots = acts.shape[1]
    capacity = slots // experts
    wide = per * rows
    f32, bf16 = jnp.float32, jnp.bfloat16
    bind = functools.partial
    sent = Sent()

    def at(q, r, s):
        return (q * cross + r) * 2 + s

    def lanes(q):
        return pl.ds(pl.multiple_of(q * wide, 128), wide)

    def copy(src, dst, send, recv, to_dp, to_expert):
        return pltpu.make_async_remote_copy(
            src_ref=src, dst_ref=dst, send_sem=send, recv_sem=recv,
            device_id=(to_dp, to_expert), device_id_type=MESH,
        )

    def y_copy(t, o):
        to = (own + o) % experts
        return copy(blocks.at[t, to], landed.at[t, own], y_send.at[t, o], y_recv.at[t, o], dp, to)

    def z_copy(k, q, step, src):
        side = 0 if step > 0 else 1
        return copy(src, fulls.at[k, at(q, x, c)], z_send.at[side, q, k], z_recv.at[q, k],
                    at(z + step, x, c), own)

    def x_copy(k, q, o, src):
        return copy(src, fulls.at[k, at(q, x, c)], x_send.at[q, o, k], x_recv.at[q, o, k],
                    at(z, (x + o) % cross, c), own)

    def c_copy(k, q, r, src):
        return copy(src, fulls.at[k, at(q, r, c)], c_send.at[q, r, k], c_recv.at[q, r, k],
                    other, own)

    greet(lines, cross, experts)
    for k in range(3):
        sent.start(bind(lambda k: z_copy(k, z, 1, shards[k]), k), z < lines - 1)
        sent.start(bind(lambda k: z_copy(k, z, -1, shards[k]), k), z > 0)
        for o in range(1, cross):
            sent.start(bind(lambda k, o: x_copy(k, z, o, shards[k]), k, o))
        sent.start(bind(lambda k: c_copy(k, z, x, shards[k]), k))
    local = [
        pltpu.make_async_copy(shards[k], fulls.at[k, dp], own_sem.at[k]) for k in range(3)
    ]
    for each in local:
        each.start()

    for t in range(2):
        def pack(q, carry, t=t):
            values = (tokens, grad_out)[t][:, lanes(q)]
            if t == 1:
                weight = levels[...].astype(f32) / 64.0
                values = (weight * values.astype(f32)).astype(bf16)
            packed = jnp.dot(to_slot[...], values, preferred_element_type=f32).astype(bf16)
            blocks[t, :, :, lanes(q)] = packed.reshape(experts, capacity, wide)
            return carry
        lax.fori_loop(0, lines, pack, 0)
        for o in range(1, experts):
            sent.start(bind(y_copy, t, o))
        landed[t, own] = blocks[t, own]
    for each in local:
        each.wait()

    def from_z(k, q, step, cond):
        held = lambda: fulls.at[k, at(q, x, c)]
        run(lambda: z_copy(k, q, step, held()).wait_recv(), cond)
        onward = (z < lines - 1) if step > 0 else (z > 0)
        sent.start(lambda: z_copy(k, q, step, held()), cond & onward)
        for o in range(1, cross):
            sent.start(bind(lambda o: x_copy(k, q, o, held()), o), cond)
        sent.start(lambda: c_copy(k, q, x, held()), cond)

    def from_x(k, q, cond):
        for o in range(1, cross):
            r = (x - o + cross) % cross
            held = bind(lambda r: fulls.at[k, at(q, r, c)], r)
            run(lambda: copy(held(), held(), x_send.at[q, o, k], x_recv.at[q, o, k], other, own).wait_recv(), cond)
            sent.start(bind(lambda r, held: c_copy(k, q, r, held()), r, held), cond)

    table = [sorted(range(lines), key=lambda q: (abs(q - p), q)) for p in range(lines)]

    def near(j):
        q = table[0][j]
        for p in range(1, lines):
            q = jnp.where(z == p, table[p][j], q)
        return q

    def slice_of(t, q):
        return landed[t, :, :, lanes(q)].reshape(slots, wide)

    def forward(j):
        q = near(j)
        for k in range(3):
            for r in range(cross):
                held = fulls.at[k, at(q, r, 1 - c)]
                copy(held, held, c_send.at[q, r, k], c_recv.at[q, r, k], other, own).wait_recv()
            weights = fulls[k, pl.ds(q * per, per)].reshape(wide, width)
            more = jnp.dot(slice_of(0 if k < 2 else 1, q), weights, preferred_element_type=f32)
            acts[k] = more if j == 0 else acts[k] + more

    done = 0
    for s in range(1, lines + 1):
        for k in range(3):
            if s < lines:
                from_z(k, z - s, 1, z >= s)
                from_z(k, z + s, -1, z + s < lines)
            if s == 1:
                from_x(k, z, None)
            else:
                from_x(k, z - (s - 1), z >= s - 1)
                from_x(k, z + (s - 1), z + s - 1 < lines)
        if s == max(1, lines // 2):
            for t in range(2):
                for o in range(1, experts):
                    held = landed.at[t, (own - o + experts) % experts]
                    copy(held, held, y_send.at[t, o], y_recv.at[t, o], dp, (own + o) % experts).wait_recv()
        if s >= max(1, lines // 2):
            last = {lines: lines, lines - 1: lines - 1}.get(s, s - 1)
            while done < last:
                forward(done)
                done += 1

    step_rows = 32

    def middle(b, carry):
        block = pl.ds(pl.multiple_of(b * step_rows, step_rows), step_rows)
        act_gate, act_up, hidden_grad = acts[0, block], acts[1, block], acts[2, block]
        sigmoid_gate = jax.nn.sigmoid(act_gate)
        silu_gate = act_gate * sigmoid_gate
        deltas[0, block] = (
            hidden_grad * act_up * sigmoid_gate * (1.0 + act_gate * (1.0 - sigmoid_gate))
        ).astype(bf16)
        deltas[1, block] = (hidden_grad * silu_gate).astype(bf16)
        deltas[2, block] = (silu_gate * act_up).astype(bf16)
        return carry

    lax.fori_loop(0, slots // step_rows, middle, 0)

    def ry_copy(t, o):
        to = (own + o) % experts
        return copy(outs.at[t, to], returned[t].at[own], ry_send.at[t, o], ry_recv.at[t, o], dp, to)

    def rc_copy(k, q, r):
        return copy(parts.at[k, at(q, r, 1 - c)], c_buf.at[k, q, r], rc_send.at[k, q, r],
                    rc_recv.at[k, q, r], other, own)

    def rx_copy(k, q, o):
        to = (x + o) % cross
        return copy(c_buf.at[k, q, to], x_buf.at[k, q, o - 1], rx_send.at[k, q, o],
                    rx_recv.at[k, q, o], at(z, to, c), own)

    def rz_copy(k, q, step):
        slot = q if step > 0 else jnp.where(q == z - 1, lines, q)
        return copy(c_buf.at[k, q, x], z_buf.at[k, slot], rz_send.at[k, q], rz_recv.at[k, slot],
                    at(z + step, x, c), own)

    def pair(k, q, r):
        rc_copy(k, q, r).wait_recv()
        return parts[k, at(q, r, c)].astype(f32) + c_buf[k, q, r].astype(f32)

    def make_parts(i):
        q = near(lines - 1 - i)
        for k in range(3):
            made = contract_first(slice_of(0 if k < 2 else 1, q), deltas[k])
            parts[k, pl.ds(q * per, per)] = made.astype(bf16).reshape(per, rows, width)
            for o in range(cross):
                sent.start(bind(lambda k, q, o: rc_copy(k, q, (x + 1 + o) % cross), k, q, o))

    def send_across(i):
        q = near(lines - 1 - i)
        for k in range(3):
            for o in range(1, cross):
                r = (x + o) % cross
                c_buf[k, q, r] = pair(k, q, r).astype(bf16)
                sent.start(bind(rx_copy, k, q, o))

    def outputs():
        def body(q, carry):
            def weights(k):
                return fulls[k, pl.ds(q * per, per)].reshape(wide, width)
            out = contract_last(deltas[2], weights(2)).astype(bf16)
            outs[0, :, :, lanes(q)] = out.reshape(experts, capacity, wide)
            grad = contract_last(deltas[0], weights(0)) + contract_last(deltas[1], weights(1))
            outs[1, :, :, lanes(q)] = grad.astype(bf16).reshape(experts, capacity, wide)
            return carry
        lax.fori_loop(0, lines, body, 0)
        for t in range(2):
            for o in range(1, experts):
                sent.start(bind(ry_copy, t, o))
        return [
            pltpu.make_async_copy(outs.at[t, own], returned[t].at[own], own_sem.at[t])
            for t in range(2)
        ]

    make_parts(0)
    for i in range(1, lines):
        make_parts(i)
        send_across(i - 1)
    send_across(lines - 1)
    local = outputs()
    for each in local:
        each.start()
    for i in range(lines):
        q = near(lines - 1 - i)
        for k in range(3):
            total = pair(k, q, x)
            for o in range(1, cross):
                rx_copy(k, q, o).wait_recv()
                total = total + x_buf[k, q, o - 1].astype(f32)
            acc[...] = total

            def add(slot, k=k):
                held = z_buf.at[k, slot]
                copy(held, held, rz_send.at[k, 0], rz_recv.at[k, slot], other, own).wait_recv()
                acc[...] += z_buf[k, slot].astype(f32)

            run(bind(add, q), (z > 0) & (q >= z))
            run(bind(add, jnp.where(q == z, lines, q)), (z < lines - 1) & (q <= z))

            def keep(k=k):
                totals[k] = acc[...]

            def pass_on(k=k, q=q):
                c_buf[k, q, x] = acc[...].astype(bf16)

            run(keep, q == z)
            run(pass_on, q != z)
            sent.start(bind(rz_copy, k, q, 1), q > z)
            sent.start(bind(rz_copy, k, q, -1), q < z)
    for t in range(2):
        for o in range(1, experts):
            held = returned[t].at[(own - o + experts) % experts]
            copy(held, held, ry_send.at[t, o], ry_recv.at[t, o], dp, (own + o) % experts).wait_recv()
    for each in local:
        each.wait()
    sent.finish()


def layer(lines, cross, experts, trio, to_slot, tokens, levels, grad_out):
    n = lines * cross * 2
    rows, width = trio[0].shape
    slots = to_slot.shape[0]
    capacity = slots // experts
    model_width = tokens.shape[1]
    dma = pltpu.SemaphoreType.DMA
    anywhere = pl.BlockSpec(memory_space=pl.ANY)
    inside = pl.BlockSpec(memory_space=pltpu.VMEM)
    bf16, f32 = jnp.bfloat16, jnp.float32
    back = jax.ShapeDtypeStruct((experts, capacity, model_width), bf16)
    pair = pltpu.VMEM((2, experts, capacity, model_width), bf16)
    by_shard = [dma((lines, cross, 3)) for _ in range(4)]
    by_part = [dma((3, lines, cross)) for _ in range(4)]
    swap = [dma((2, experts)), dma((2, experts))]
    totals, returned, arrived = pl.pallas_call(
        functools.partial(layer_kernel, lines, cross, experts),
        out_shape=[jax.ShapeDtypeStruct((3, rows, width), f32), back, back],
        in_specs=[anywhere] * 3 + [inside] * 4,
        out_specs=[inside, anywhere, anywhere],
        scratch_shapes=[
            pltpu.VMEM((3, n, rows, width), bf16),
            pair, pair, pair,
            pltpu.VMEM((3, slots, width), f32),
            pltpu.VMEM((3, slots, width), bf16),
            pltpu.VMEM((3, n, rows, width), bf16),
            pltpu.VMEM((3, lines, cross, rows, width), bf16),
            pltpu.VMEM((3, lines, max(1, cross - 1), rows, width), bf16),
            pltpu.VMEM((3, lines + 1, rows, width), bf16),
            pltpu.VMEM((rows, width), f32),
            dma((2, lines, 3)), dma((lines, 3)), *by_shard, *swap, dma((3,)),
            dma((3, lines)), dma((3, lines + 1)), *by_part, *swap,
        ],
        compiler_params=pltpu.CompilerParams(
            collective_id=0, has_side_effects=True, vmem_limit_bytes=VMEM_LIMIT
        ),
        name="expert_layer",
    )(*trio, to_slot, tokens, levels, grad_out)
    return totals, returned, arrived


def shards(lines, cross, tokens, routes, gate_levels, w_gate, w_up, w_down, grad_out):
    experts = lax.axis_size("expert")
    tok_rows = tokens.shape[0]
    model_width = tokens.shape[1]
    capacity = min(tok_rows, tok_rows * TOP * 5 // (4 * experts))
    capacity = -(-capacity // 16) * 16
    slot_count = experts * capacity
    expert_of = routes[:, 0]
    onehot = (expert_of[:, None] == jnp.arange(experts, dtype=jnp.int32)[None, :]).astype(jnp.bfloat16)
    place = jnp.arange(tok_rows, dtype=jnp.int32)
    earlier = jnp.dot(
        (place[:, None] > place[None, :]).astype(jnp.bfloat16), onehot,
        preferred_element_type=jnp.float32,
    )
    slot_rank = jnp.sum(earlier * onehot.astype(jnp.float32), axis=1).astype(jnp.int32)
    slot_index = expert_of * capacity + slot_rank
    to_slot = (slot_index[:, None] == jnp.arange(slot_count, dtype=jnp.int32)[None, :]).astype(
        jnp.bfloat16
    )
    gate_weight = gate_levels.astype(jnp.float32) / 64.0

    def unpack_rows(values):
        return jnp.dot(
            to_slot, values.reshape(slot_count, model_width), preferred_element_type=jnp.float32
        )

    totals, returned, arrived = layer(
        lines, cross, experts, (w_gate[0], w_up[0], w_down[0]),
        to_slot.T, tokens, gate_levels, grad_out,
    )
    moe_out = (gate_weight * unpack_rows(returned)).astype(jnp.bfloat16)
    grad_tokens = unpack_rows(arrived).astype(jnp.bfloat16)
    return (moe_out, grad_tokens, totals[0:1], totals[1:2], totals[2:3])


def solution(mesh):
    chips = mesh.shape["dp"] // 2
    lines = 4 if chips % 4 == 0 else chips
    in_specs = (
        P(("dp", "expert"), None),
        P(("dp", "expert"), None),
        P(("dp", "expert"), None),
        P("expert", "dp", None),
        P("expert", "dp", None),
        P("expert", "dp", None),
        P(("dp", "expert"), None),
    )
    out_specs = (
        P(("dp", "expert"), None),
        P(("dp", "expert"), None),
        P("expert", "dp", None),
        P("expert", "dp", None),
        P("expert", "dp", None),
    )
    return jax.shard_map(
        functools.partial(shards, lines, chips // lines),
        mesh=mesh, in_specs=in_specs, out_specs=out_specs, check_vma=False,
    )
```

```python
import functools

import jax
import jax.numpy as jnp
from jax import lax
from jax.experimental import pallas as pl
from jax.experimental.pallas import tpu as pltpu
from jax.sharding import PartitionSpec as P

TOP = 1
MESH = pl.DeviceIdType.MESH
VMEM_LIMIT = 62 * 1024 * 1024


def contract_last(matrix_a, matrix_b):
    return lax.dot_general(
        matrix_a, matrix_b, (((1,), (1,)), ((), ())), preferred_element_type=jnp.float32
    )


def contract_first(matrix_a, matrix_b):
    return lax.dot_general(
        matrix_a, matrix_b, (((0,), (0,)), ((), ())), preferred_element_type=jnp.float32
    )


class Sent:
    def __init__(self):
        self.made = []

    def start(self, make, cond=None):
        self.made.append((make, cond))
        run(lambda: make().start(), cond)

    def finish(self):
        for make, cond in self.made:
            run(lambda make=make: make().wait_send(), cond)


def run(body, cond=None):
    if cond is None:
        body()
    else:
        pl.when(cond)(body)


def places(lines, cross):
    dp = lax.axis_index("dp")
    return dp, lax.axis_index("expert"), dp // (2 * cross), (dp // 2) % cross, dp % 2


def greet(lines, cross, experts):
    dp, own, z, x, c = places(lines, cross)
    barrier = pltpu.get_barrier_semaphore()

    def hello(to_dp, to_expert):
        pl.semaphore_signal(barrier, inc=1, device_id=(to_dp, to_expert), device_id_type=MESH)

    run(lambda: hello(dp + 2 * cross, own), z < lines - 1)
    run(lambda: hello(dp - 2 * cross, own), z > 0)
    for o in range(1, cross):
        hello((z * cross + (x + o) % cross) * 2 + c, own)
    hello(dp + 1 - 2 * c, own)
    for o in range(1, experts):
        hello(dp, (own + o) % experts)
    up = jnp.where(z < lines - 1, 1, 0)
    down = jnp.where(z > 0, 1, 0)
    pl.semaphore_wait(barrier, up + down + (cross - 1) + 1 + (experts - 1))


def layer_kernel(lines, cross, experts, *refs):
    shards, routes, levels, tokens, grad_out = refs[0:3], refs[3], refs[4], refs[5], refs[6]
    totals, rows_out = refs[7], refs[8:10]
    fulls, blocks, landed, returned, to_slot, acts, deltas, parts, c_buf, x_buf, z_buf, acc = refs[10:22]
    (z_send, z_recv, x_send, x_recv, c_send, c_recv, y_send, y_recv, own_sem,
     rz_send, rz_recv, rx_send, rx_recv, rc_send, rc_recv, ry_send, ry_recv) = refs[22:]
    dp, own, z, x, c = places(lines, cross)
    other = dp + 1 - 2 * c
    per = 2 * cross
    rows, width = fulls.shape[2], fulls.shape[3]
    slots = acts.shape[1]
    capacity = slots // experts
    wide = per * rows
    f32, bf16 = jnp.float32, jnp.bfloat16
    bind = functools.partial
    sent = Sent()

    def at(q, r, s):
        return (q * cross + r) * 2 + s

    def lanes(q):
        return pl.ds(pl.multiple_of(q * wide, 128), wide)

    def copy(src, dst, send, recv, to_dp, to_expert):
        return pltpu.make_async_remote_copy(
            src_ref=src, dst_ref=dst, send_sem=send, recv_sem=recv,
            device_id=(to_dp, to_expert), device_id_type=MESH,
        )

    def y_copy(t, o):
        to = (own + o) % experts
        return copy(blocks.at[t, to], landed.at[t, own], y_send.at[t, o], y_recv.at[t, o], dp, to)

    def z_copy(k, q, step, src):
        side = 0 if step > 0 else 1
        return copy(src, fulls.at[k, at(q, x, c)], z_send.at[side, q, k], z_recv.at[q, k],
                    at(z + step, x, c), own)

    def x_copy(k, q, o, src):
        return copy(src, fulls.at[k, at(q, x, c)], x_send.at[q, o, k], x_recv.at[q, o, k],
                    at(z, (x + o) % cross, c), own)

    def c_copy(k, q, r, src):
        return copy(src, fulls.at[k, at(q, r, c)], c_send.at[q, r, k], c_recv.at[q, r, k],
                    other, own)

    greet(lines, cross, experts)
    for k in range(3):
        sent.start(bind(lambda k: z_copy(k, z, 1, shards[k]), k), z < lines - 1)
        sent.start(bind(lambda k: z_copy(k, z, -1, shards[k]), k), z > 0)
        for o in range(1, cross):
            sent.start(bind(lambda k, o: x_copy(k, z, o, shards[k]), k, o))
        sent.start(bind(lambda k: c_copy(k, z, x, shards[k]), k))
    local = [
        pltpu.make_async_copy(shards[k], fulls.at[k, dp], own_sem.at[k]) for k in range(3)
    ]
    for each in local:
        each.start()

    tok_rows = tokens.shape[0]
    expert_row = routes[...]
    some = (max(16, experts), tok_rows)
    chosen = (lax.broadcasted_iota(jnp.int32, some, 0) == expert_row).astype(f32)
    square = (tok_rows, tok_rows)
    before = lax.broadcasted_iota(jnp.int32, square, 0) < lax.broadcasted_iota(jnp.int32, square, 1)
    earlier = jnp.dot(chosen.astype(bf16), before.astype(f32).astype(bf16), preferred_element_type=f32)
    rank = jnp.sum(earlier * chosen, axis=0, keepdims=True).astype(jnp.int32)
    slot = expert_row * capacity + rank
    placed = (lax.broadcasted_iota(jnp.int32, (slots, tok_rows), 0) == slot).astype(f32)
    to_slot[0] = placed.astype(bf16)
    to_slot[1] = (placed * (levels[...].astype(f32) / 64.0)).astype(bf16)

    for t in range(2):
        def pack(q, carry, t=t):
            values = (tokens, grad_out)[t][:, lanes(q)]
            packed = jnp.dot(to_slot[t], values, preferred_element_type=f32).astype(bf16)
            blocks[t, :, :, lanes(q)] = packed.reshape(experts, capacity, wide)
            return carry
        lax.fori_loop(0, lines, pack, 0)
        for o in range(1, experts):
            y_copy(t, o).start()
        landed[t, own] = blocks[t, own]
    for each in local:
        each.wait()

    def from_z(k, q, step, cond):
        held = lambda: fulls.at[k, at(q, x, c)]
        run(lambda: z_copy(k, q, step, held()).wait_recv(), cond)
        onward = (z < lines - 1) if step > 0 else (z > 0)
        sent.start(lambda: z_copy(k, q, step, held()), cond & onward)
        for o in range(1, cross):
            sent.start(bind(lambda o: x_copy(k, q, o, held()), o), cond)
        sent.start(lambda: c_copy(k, q, x, held()), cond)

    def from_x(k, q, cond):
        for o in range(1, cross):
            r = (x - o + cross) % cross
            held = bind(lambda r: fulls.at[k, at(q, r, c)], r)
            run(lambda: copy(held(), held(), x_send.at[q, o, k], x_recv.at[q, o, k], other, own).wait_recv(), cond)
            sent.start(bind(lambda r, held: c_copy(k, q, r, held()), r, held), cond)

    table = [sorted(range(lines), key=lambda q: (abs(q - p), q)) for p in range(lines)]

    def near(j):
        q = table[0][j]
        for p in range(1, lines):
            q = jnp.where(z == p, table[p][j], q)
        return q

    def slice_of(t, q):
        return landed[t, :, :, lanes(q)].reshape(slots, wide)

    def forward(j, kinds):
        q = near(j)
        for k in kinds:
            for r in range(cross):
                held = fulls.at[k, at(q, r, 1 - c)]
                copy(held, held, c_send.at[q, r, k], c_recv.at[q, r, k], other, own).wait_recv()
            weights = fulls[k, pl.ds(q * per, per)].reshape(wide, width)
            more = jnp.dot(slice_of(0 if k < 2 else 1, q), weights, preferred_element_type=f32)
            acts[k] = more if j == 0 else acts[k] + more

    def y_arrived(t):
        for o in range(1, experts):
            held = landed.at[t, (own - o + experts) % experts]
            copy(held, held, y_send.at[t, o], y_recv.at[t, o], dp, (own + o) % experts).wait_recv()

    def gather_step(s, kinds):
        for k in kinds:
            if s < lines:
                from_z(k, z - s, 1, z >= s)
                from_z(k, z + s, -1, z + s < lines)
            if s == 1:
                from_x(k, z, None)
            else:
                from_x(k, z - (s - 1), z >= s - 1)
                from_x(k, z + (s - 1), z + s - 1 < lines)

    done = 0
    for s in range(1, lines + 1):
        gather_step(s, (0, 1))
        if s == max(1, lines // 2):
            y_arrived(0)
        if s >= max(1, lines // 2):
            last = {lines: lines, lines - 1: lines - 1}.get(s, s - 1)
            while done < last:
                forward(done, (0, 1))
                done += 1
    y_arrived(1)

    step_rows = 32

    def block_of(b):
        return pl.ds(pl.multiple_of(b * step_rows, step_rows), step_rows)

    def make_hidden(b, carry):
        act_gate, act_up = acts[0, block_of(b)], acts[1, block_of(b)]
        deltas[2, block_of(b)] = (act_gate * jax.nn.sigmoid(act_gate) * act_up).astype(bf16)
        return carry

    def make_deltas(b, carry):
        act_gate, act_up, hidden_grad = (acts[k, block_of(b)] for k in range(3))
        sigmoid_gate = jax.nn.sigmoid(act_gate)
        silu_gate = act_gate * sigmoid_gate
        deltas[0, block_of(b)] = (
            hidden_grad * act_up * sigmoid_gate * (1.0 + act_gate * (1.0 - sigmoid_gate))
        ).astype(bf16)
        deltas[1, block_of(b)] = (hidden_grad * silu_gate).astype(bf16)
        return carry

    def ry_copy(t, o):
        to = (own + o) % experts
        return copy(blocks.at[t, to], returned.at[t, own], ry_send.at[t, o], ry_recv.at[t, o], dp, to)

    def rc_copy(k, q, r):
        return copy(parts.at[k, at(q, r, 1 - c)], c_buf.at[k, q, r], rc_send.at[k, q, r],
                    rc_recv.at[k, q, r], other, own)

    def rx_copy(k, q, o):
        to = (x + o) % cross
        return copy(c_buf.at[k, q, to], x_buf.at[k, q, o - 1], rx_send.at[k, q, o],
                    rx_recv.at[k, q, o], at(z, to, c), own)

    def rz_copy(k, q, step):
        slot = q if step > 0 else jnp.where(q == z - 1, lines, q)
        return copy(c_buf.at[k, q, x], z_buf.at[k, slot], rz_send.at[k, q], rz_recv.at[k, slot],
                    at(z + step, x, c), own)

    def pair(k, q, r):
        rc_copy(k, q, r).wait_recv()
        return parts[k, at(q, r, c)].astype(f32) + c_buf[k, q, r].astype(f32)

    def make_parts(i, kinds):
        q = near(lines - 1 - i)
        for k in kinds:
            made = contract_first(slice_of(0 if k < 2 else 1, q), deltas[k])
            parts[k, pl.ds(q * per, per)] = made.astype(bf16).reshape(per, rows, width)
            for o in range(cross):
                sent.start(bind(lambda k, q, o: rc_copy(k, q, (x + 1 + o) % cross), k, q, o))

    def send_across(i, kinds):
        q = near(lines - 1 - i)
        for k in kinds:
            for o in range(1, cross):
                r = (x + o) % cross
                c_buf[k, q, r] = pair(k, q, r).astype(bf16)
                sent.start(bind(rx_copy, k, q, o))

    def outputs():
        for t in range(2):
            for o in range(1, experts):
                y_copy(t, o).wait_send()

        def body(q, carry):
            def weights(k):
                return fulls[k, pl.ds(q * per, per)].reshape(wide, width)
            out = contract_last(deltas[2], weights(2)).astype(bf16)
            blocks[0, :, :, lanes(q)] = out.reshape(experts, capacity, wide)
            grad = contract_last(deltas[0], weights(0)) + contract_last(deltas[1], weights(1))
            blocks[1, :, :, lanes(q)] = grad.astype(bf16).reshape(experts, capacity, wide)
            return carry
        lax.fori_loop(0, lines, body, 0)
        for t in range(2):
            for o in range(1, experts):
                sent.start(bind(ry_copy, t, o))
            returned[t, own] = blocks[t, own]

    def unpack(t):
        for o in range(1, experts):
            held = returned.at[t, (own - o + experts) % experts]
            copy(held, held, ry_send.at[t, o], ry_recv.at[t, o], dp, (own + o) % experts).wait_recv()

        def body(q, carry):
            values = returned[t, :, :, lanes(q)].reshape(slots, wide)
            rows_out[t][:, lanes(q)] = contract_first(to_slot[1 - t], values).astype(bf16)
            return carry
        lax.fori_loop(0, lines, body, 0)

    def along(i, k):
        q = near(lines - 1 - i)
        total = pair(k, q, x)
        for o in range(1, cross):
            rx_copy(k, q, o).wait_recv()
            total = total + x_buf[k, q, o - 1].astype(f32)
        acc[...] = total

        def add(slot):
            held = z_buf.at[k, slot]
            copy(held, held, rz_send.at[k, 0], rz_recv.at[k, slot], other, own).wait_recv()
            acc[...] += z_buf[k, slot].astype(f32)

        run(bind(add, q), (z > 0) & (q >= z))
        run(bind(add, jnp.where(q == z, lines, q)), (z < lines - 1) & (q <= z))

        def keep():
            totals[k] = acc[...]

        def pass_on():
            c_buf[k, q, x] = acc[...].astype(bf16)

        run(keep, q == z)
        run(pass_on, q != z)
        sent.start(bind(rz_copy, k, q, 1), q > z)
        sent.start(bind(rz_copy, k, q, -1), q < z)

    lax.fori_loop(0, slots // step_rows, make_hidden, 0)
    for s in range(1, lines + 1):
        gather_step(s, (2,))
        make_parts(s - 1, (2,))
        if s > 1:
            send_across(s - 2, (2,))
    send_across(lines - 1, (2,))
    for j in range(lines):
        forward(j, (2,))
    lax.fori_loop(0, slots // step_rows, make_deltas, 0)
    make_parts(0, (0, 1))
    for i in range(1, lines):
        make_parts(i, (0, 1))
        send_across(i - 1, (0, 1))
    send_across(lines - 1, (0, 1))
    outputs()
    for i in range(lines):
        along(i, 2)
    for i in range(lines):
        for k in (0, 1):
            along(i, k)
        if i == max(0, lines - 3):
            unpack(0)
        if i == max(0, lines - 2):
            unpack(1)
    sent.finish()


def layer(lines, cross, experts, capacity, trio, routes, levels, tokens, grad_out):
    n = lines * cross * 2
    rows, width = trio[0].shape
    slots = experts * capacity
    tok_rows, model_width = tokens.shape
    dma = pltpu.SemaphoreType.DMA
    anywhere = pl.BlockSpec(memory_space=pl.ANY)
    inside = pl.BlockSpec(memory_space=pltpu.VMEM)
    bf16, f32 = jnp.bfloat16, jnp.float32
    back = jax.ShapeDtypeStruct((tok_rows, model_width), bf16)
    pair = pltpu.VMEM((2, experts, capacity, model_width), bf16)
    by_shard = [dma((lines, cross, 3)) for _ in range(4)]
    by_part = [dma((3, lines, cross)) for _ in range(4)]
    swap = [dma((2, experts)), dma((2, experts))]
    return pl.pallas_call(
        functools.partial(layer_kernel, lines, cross, experts),
        out_shape=[jax.ShapeDtypeStruct((3, rows, width), f32), back, back],
        in_specs=[anywhere] * 3 + [inside] * 4,
        out_specs=[inside] * 3,
        scratch_shapes=[
            pltpu.VMEM((3, n, rows, width), bf16),
            pair, pair, pair,
            pltpu.VMEM((2, slots, tok_rows), bf16),
            pltpu.VMEM((3, slots, width), f32),
            pltpu.VMEM((3, slots, width), bf16),
            pltpu.VMEM((3, n, rows, width), bf16),
            pltpu.VMEM((3, lines, cross, rows, width), bf16),
            pltpu.VMEM((3, lines, max(1, cross - 1), rows, width), bf16),
            pltpu.VMEM((3, lines + 1, rows, width), bf16),
            pltpu.VMEM((rows, width), f32),
            dma((2, lines, 3)), dma((lines, 3)), *by_shard, *swap, dma((3,)),
            dma((3, lines)), dma((3, lines + 1)), *by_part, *swap,
        ],
        compiler_params=pltpu.CompilerParams(
            collective_id=0, has_side_effects=True, vmem_limit_bytes=VMEM_LIMIT
        ),
        name="expert_layer",
    )(*trio, routes, levels, tokens, grad_out)


def shards(lines, cross, tokens, routes, gate_levels, w_gate, w_up, w_down, grad_out):
    experts = lax.axis_size("expert")
    tok_rows = tokens.shape[0]
    capacity = min(tok_rows, tok_rows * TOP * 5 // (4 * experts))
    capacity = -(-capacity // 16) * 16
    totals, moe_out, grad_tokens = layer(
        lines, cross, experts, capacity, (w_gate[0], w_up[0], w_down[0]),
        routes.reshape(1, tok_rows), gate_levels.reshape(1, tok_rows), tokens, grad_out,
    )
    return (moe_out, grad_tokens, totals[0:1], totals[1:2], totals[2:3])


def solution(mesh):
    chips = mesh.shape["dp"] // 2
    lines = 4 if chips % 4 == 0 else chips
    in_specs = (
        P(("dp", "expert"), None),
        P(("dp", "expert"), None),
        P(("dp", "expert"), None),
        P("expert", "dp", None),
        P("expert", "dp", None),
        P("expert", "dp", None),
        P(("dp", "expert"), None),
    )
    out_specs = (
        P(("dp", "expert"), None),
        P(("dp", "expert"), None),
        P("expert", "dp", None),
        P("expert", "dp", None),
        P("expert", "dp", None),
    )
    return jax.shard_map(
        functools.partial(shards, lines, chips // lines),
        mesh=mesh, in_specs=in_specs, out_specs=out_specs, check_vma=False,
    )
```
